256 devices in a mesh: out: 16 (over y, x_hi, core), inp: 16 (over x_lo, z).
Axes of the slice: x: 4 (x_hi: 2, x_lo: 2; x = x_hi * 2 + x_lo), y: 4, z: 8, core: 2. Of those that a mesh axis runs over, the one named last changes fastest.
Arguments:
- acts: bfloat16 [4096, 28672], P('out', 'inp'), may hold values from -6 to 6
- grads: bfloat16 [4096, 8192], P('out', 'inp'), may hold values from -6 to 6
- basis_in: bfloat16 [28672, 28672], P('inp', 'out'), may hold values from -0.03125 to 0.03125
- basis_out: bfloat16 [8192, 8192], P('inp', 'out'), may hold values from -0.0625 to 0.0625
- query_in: bfloat16 [28672, 512], P('out', 'inp'), may hold values from -0.03125 to 0.03125
- query_out: bfloat16 [8192, 512], P('out', 'inp'), may hold values from -0.0625 to 0.0625
- lengths: int32 [16], replicated, may hold values from 1 to 512, 4096 in all
Outputs:
- scores: float32 [16, 16], P(None, 'inp')
The draws below stay inside these ranges and needn't reach their ends.
Inputs may be any that keep to these rules, and one draw needn't show every extreme that they name: Each example has at least one token, the lengths sum to 4096, and the longest has exactly 512 tokens.
All inputs are finite; a program needn't handle non-finite values.
Results may differ from the reference program's by a relative error of at most 0.0003.
Values may be sent and summed in bfloat16 or wider, within the bound.
No kernel may reach another device: no remote copies, remote signals or barrier semaphores. Data moves between devices by JAX's collectives and lax.ppermute only.
A program may use at most 64 MiB of HBM per device.

```python
import math
import jax
import jax.numpy as jnp
import numpy as np
from jax import lax

INP = 28672
OUT = 8192
RANK = 32
NQ = 16
EXAMPLES = 16
TOKENS = 4096
QR = 512


def block_scale(rng, dims, cuts, low, largest):
    factor_of = 1.0
    for dim, blocks in cuts:
        draws = jax.random.uniform(jax.random.fold_in(jax.random.fold_in(rng, 6), dim), (blocks,), jnp.float32, low / len(cuts), largest / len(cuts))
        factor_of = factor_of * jnp.repeat(jnp.exp(draws), dims[dim] // blocks).reshape((-1,) + (1,) * (len(dims) - 1 - dim))
    return factor_of


def profile(count, total, limit, lean):
    loads = [(1 << 20) // math.isqrt(grade ** lean) + 1 for grade in range(2, count + 1)]
    surplus, holding = total - limit - (count - 1), [1] * (count - 1)
    while surplus > 0:
        free = [i for i in range(count - 1) if holding[i] < limit]
        mass, left = sum([loads[i] for i in free]), surplus
        for i in free:
            extra = min(limit - holding[i], max(1, left * loads[i] // mass), surplus)
            holding[i] = holding[i] + extra
            surplus = surplus - extra
    return np.array([limit] + holding)


def uneven_parts(rng, amount, total, limit, lean):
    if amount == 2:
        one = jax.random.randint(rng, (), max(1, total - limit), min(limit, total - 1) + 1)
        return jnp.stack([one, total - one])
    sizes = jnp.asarray(profile(amount, total, limit, lean), jnp.int32)
    twos = (amount - 1) // 2
    giver, taker = sizes[1:1 + 2 * twos:2], sizes[2:2 + 2 * twos:2]
    margin = jnp.minimum(giver - 1, limit - taker)
    moved = jax.random.randint(jax.random.fold_in(rng, 1), (twos,), 0, 1 << 20) % (margin + 1)
    sizes = sizes.at[1:1 + 2 * twos:2].set(giver - moved).at[2:2 + 2 * twos:2].set(taker + moved)
    return sizes[jax.random.permutation(jax.random.fold_in(rng, 2), amount)]


def scatter_about(stream_key, shape, spread, most, split=(), kind=jnp.bfloat16):
    array = spread * jax.random.normal(stream_key, shape, jnp.float32)
    if split:
        array = array * block_scale(stream_key, shape, split, -0.22, 0.18)
    return jnp.clip(array, -most, most).astype(kind)


def setup_inputs(seed: int = 0) -> dict:
    keys = jax.random.split(jax.random.key(seed), 8)
    acts = scatter_about(keys[0], (TOKENS, INP), 1.0, 6.0, ((0, 16), (1, 16)))
    grads = scatter_about(keys[1], (TOKENS, OUT), 1.0, 6.0, ((0, 16), (1, 16)))
    basis_in = scatter_about(keys[2], (INP, INP), INP ** -0.5, 0.03125, ((0, 16), (1, 16)))
    basis_out = scatter_about(keys[3], (OUT, OUT), OUT ** -0.5, 0.0625, ((0, 16), (1, 16)))
    query_in = scatter_about(keys[4], (INP, QR), INP ** -0.5, 0.03125, ((0, 16), (1, 16)))
    query_out = scatter_about(keys[5], (OUT, QR), OUT ** -0.5, 0.0625, ((0, 16), (1, 16)))
    lengths = uneven_parts(keys[6], EXAMPLES, TOKENS, TOKENS // 8, 1).astype(jnp.int32)
    return {"acts": acts, "grads": grads, "basis_in": basis_in, "basis_out": basis_out, "query_in": query_in, "query_out": query_out, "lengths": lengths}


def reference(acts, grads, basis_in, basis_out, query_in, query_out, lengths):
    rotated_in = jnp.dot(basis_in, query_in, preferred_element_type=jnp.float32)
    rotated_out = jnp.dot(basis_out, query_out, preferred_element_type=jnp.float32)
    input_side = jnp.dot(acts.astype(jnp.float32), rotated_in, precision=lax.Precision.HIGHEST)
    output_side = jnp.dot(grads.astype(jnp.float32), rotated_out, precision=lax.Precision.HIGHEST)
    per_token = jnp.sum((input_side * output_side).reshape(TOKENS, NQ, RANK), axis=2)
    finish = jnp.cumsum(lengths).astype(jnp.int32)
    starts = finish - lengths
    position = jnp.arange(TOKENS, dtype=jnp.int32)
    member = ((position[None, :] >= starts[:, None]) & (position[None, :] < finish[:, None])).astype(jnp.float32)
    summed = jnp.dot(member, per_token, precision=lax.Precision.HIGHEST)
    return summed / lengths.astype(jnp.float32)[:, None]
```

```python
import functools

import jax
import jax.numpy as jnp
from jax import lax
from jax.experimental import pallas as pl
from jax.experimental.pallas import tpu as pltpu
from jax.sharding import PartitionSpec as P

RANK = 32
LEVELS = 32700.0
STEPS = 64.0
PAD = 128
VMEM = pl.BlockSpec(memory_space=pltpu.VMEM)
SMEM = pl.BlockSpec(memory_space=pltpu.SMEM)


def params(mib):
    return pltpu.CompilerParams(vmem_limit_bytes=mib << 20)


def core_id():
    return lax.rem(lax.axis_index("out"), 2)


def level_of(x):
    largest = jnp.max(jnp.abs(x), axis=1, keepdims=True)
    return jnp.ceil(jnp.log2(jnp.maximum(largest, 1e-30)) * STEPS)


def encode(x, level):
    scaled = x * (jnp.exp2(level * (-1.0 / STEPS)) * LEVELS)
    scaled = jnp.clip(scaled, -32767.0, 32767.0)
    return jnp.round(scaled).astype(jnp.int32).astype(jnp.int16)


def unit_of(level):
    return jnp.exp2(level * (1.0 / STEPS)) * (1.0 / LEVELS)


def pack_levels(level_in, level_out):
    rows = level_in.shape[0]
    lane = lax.broadcasted_iota(jnp.int32, (rows, PAD), 1)
    both = jnp.where(lane < PAD // 2, level_in, level_out)
    return both.astype(jnp.int32).astype(jnp.int16)


def as_float(x):
    return x.astype(jnp.int32).astype(jnp.float32)


def units(tail):
    tail = as_float(tail)
    return unit_of(tail[:, 0:1]), unit_of(tail[:, PAD // 2 : PAD // 2 + 1])


def rotate_kernel(in_tiles, a_ref, b_ref, basis_in, basis_out, keep, send):
    step = pl.program_id(0)
    first = core_id() == 0
    width = basis_in.shape[1]
    contract = (((1,), (1,)), ((), ()))

    def run(lo, hi, basis):
        a, b = a_ref[:, lo:hi], b_ref[:, lo:hi]
        rows = jnp.concatenate([jnp.where(first, a, b), jnp.where(first, b, a)], axis=0)
        got = lax.dot_general(rows, basis[...], contract, preferred_element_type=jnp.float32)
        half = a.shape[0]
        keep[...] = got[:half]
        send[...] = got[half:]

    @pl.when(step < in_tiles)
    def _():
        run(0, width, basis_in)

    @pl.when(step >= in_tiles)
    def _():
        run(width, width + basis_out.shape[1], basis_out)


def rotate(a, b, basis_in, basis_out):
    tile = 256
    rows, width = a.shape
    in_tiles, out_tiles = basis_in.shape[0] // tile, basis_out.shape[0] // tile
    whole = pl.BlockSpec((rows, width), lambda i: (0, 0))
    result = pl.BlockSpec((rows, tile), lambda i: (0, i))
    shape = jax.ShapeDtypeStruct((rows, width), jnp.float32)
    flops = 4 * rows * (basis_in.size + basis_out.size)
    return pl.pallas_call(
        functools.partial(rotate_kernel, in_tiles),
        grid=(in_tiles + out_tiles,),
        in_specs=[
            whole,
            whole,
            pl.BlockSpec((tile, basis_in.shape[1]), lambda i: (jnp.minimum(i, in_tiles - 1), 0)),
            pl.BlockSpec((tile, basis_out.shape[1]), lambda i: (jnp.maximum(i - in_tiles, 0), 0)),
        ],
        out_specs=[result, result],
        out_shape=[shape, shape],
        compiler_params=params(24),
        cost_estimate=pl.CostEstimate(
            flops=flops, bytes_accessed=2 * basis_in.size + 2 * basis_out.size, transcendentals=0
        ),
    )(a, b, basis_in, basis_out)


def store_codes(total, in_width, store):
    side_in, side_out = total[:, :in_width], total[:, in_width:]
    level_in, level_out = level_of(side_in), level_of(side_out)
    store(0, in_width, encode(side_in, level_in))
    store(in_width, total.shape[1], encode(side_out, level_out))
    store(total.shape[1], total.shape[1] + PAD, pack_levels(level_in, level_out))


def code_kernel(in_width, *refs):
    keeps, gots, out = refs[:5], refs[5:10], refs[10]
    slot = 0
    for keep, got in zip(keeps, gots):
        for part in range(keep.shape[0] // RANK):
            rows = slice(part * RANK, (part + 1) * RANK)

            def store(lo, hi, value, slot=slot):
                out[slot, :, lo:hi] = value

            store_codes(keep[rows] + got[rows], in_width, store)
            slot += 1


def code(keeps, gots, in_width):
    width = keeps[0].shape[1]
    return pl.pallas_call(
        functools.partial(code_kernel, in_width),
        in_specs=[VMEM] * 10,
        out_specs=VMEM,
        out_shape=jax.ShapeDtypeStruct((8, RANK, width + PAD), jnp.int16),
        compiler_params=params(40),
    )(*keeps, *gots)


def resum_kernel(in_width, codes, out):
    width = codes.shape[2] - PAD
    total_in = total_out = 0.0
    for source in range(codes.shape[0]):
        unit_in, unit_out = units(codes[source, :, width:])
        total_in += as_float(codes[source, :, :in_width]) * unit_in
        total_out += as_float(codes[source, :, in_width:width]) * unit_out

    def store(lo, hi, value):
        for target in range(out.shape[0]):
            out[target, :, lo:hi] = value

    store_codes(jnp.concatenate([total_in, total_out], axis=1), in_width, store)


def resum(codes, in_width):
    return pl.pallas_call(
        functools.partial(resum_kernel, in_width),
        in_specs=[VMEM],
        out_specs=VMEM,
        out_shape=jax.ShapeDtypeStruct(codes.shape, jnp.int16),
        compiler_params=params(24),
    )(codes)


def project_kernel(own, other, acts, grads, out):
    core = core_id()
    place = lax.axis_index("inp")
    x_lo, z = place // 8, lax.rem(place, 8)
    in_width, tokens = acts.shape[1], acts.shape[0]
    width = own.shape[2] - PAD
    contract = (((1,), (1,)), ((), ()))

    def side(codes, unit, data):
        value = as_float(codes)
        high = value.astype(jnp.bfloat16)
        low = (value - high.astype(jnp.float32)).astype(jnp.bfloat16)
        data = data[...]
        got = lax.dot_general(high, data, contract, preferred_element_type=jnp.float32)
        got += lax.dot_general(low, data, contract, preferred_element_type=jnp.float32)
        return got * unit

    for codes, half in ((own, core), (other, 1 - core)):
        rows = codes.shape[0] * RANK
        unit_in, unit_out = units(codes[:, :, width:].reshape(rows, PAD))
        side_in = side(codes[:, :, :in_width].reshape(rows, in_width), unit_in, acts)
        side_out = side(codes[:, :, in_width:width].reshape(rows, width - in_width), unit_out, grads)
        level_in, level_out = level_of(side_in), level_of(side_out)
        code_in, code_out = encode(side_in, level_in), encode(side_out, level_out)
        tail = pack_levels(level_in, level_out)
        sign = 2 * half - 1
        for slot in range(8):
            away = (slot + 1) // 2
            cross = (slot + 1) % 2 if 0 < slot < 7 else half
            target = lax.rem(x_lo + cross, 2) * 8 + lax.rem(z + sign * away + 8, 8)
            span = slice(slot * RANK, (slot + 1) * RANK)
            out[target, :, 0:tokens] = code_in[span]
            out[target, :, tokens : 2 * tokens] = code_out[span]
            out[target, :, 2 * tokens :] = tail[span]


def project(own, other, acts, grads):
    tokens = acts.shape[0]
    return pl.pallas_call(
        project_kernel,
        in_specs=[VMEM] * 4,
        out_specs=VMEM,
        out_shape=jax.ShapeDtypeStruct((16, RANK, 2 * tokens + PAD), jnp.int16),
        compiler_params=params(40),
    )(own, other, acts, grads)


def score_kernel(lengths, codes, out):
    tokens = (codes.shape[2] - PAD) // 2
    side_in = side_out = 0.0
    for source in range(codes.shape[0]):
        unit_in, unit_out = units(codes[source, :, 2 * tokens :])
        side_in += as_float(codes[source, :, :tokens]) * unit_in
        side_out += as_float(codes[source, :, tokens : 2 * tokens]) * unit_out
    per_token = jnp.sum(side_in * side_out, axis=0, keepdims=True)
    position = lax.axis_index("out") * tokens + lax.broadcasted_iota(jnp.int32, (1, tokens), 1)
    lane = lax.broadcasted_iota(jnp.int32, (1, 128), 1)
    sums = jnp.zeros((1, 128), jnp.float32)
    start = jnp.int32(0)
    for example in range(lengths.shape[0]):
        finish = start + lengths[example]
        inside = (position >= start) & (position < finish)
        total = jnp.sum(jnp.where(inside, per_token, 0.0), axis=1, keepdims=True)
        sums = jnp.where(lane == example, total, sums)
        start = finish
    for target in range(out.shape[0]):
        out[target] = jnp.broadcast_to(sums, out.shape[1:])


def score(lengths, codes):
    return pl.pallas_call(
        score_kernel,
        in_specs=[SMEM, VMEM],
        out_specs=VMEM,
        out_shape=jax.ShapeDtypeStruct((16, 8, 128), jnp.float32),
        compiler_params=params(16),
    )(lengths, codes)


UP = [(x * 8 + z, x * 8 + (z + 1) % 8) for x in range(2) for z in range(8)]
DOWN = [(b, a) for a, b in UP]
ACROSS = [(i, (i + 8) % 16) for i in range(16)]
CORES = [(i, i ^ 1) for i in range(16)]
CHIPS = [[2 * chip + core for chip in range(8)] for core in range(2)]


def per_device(acts, grads, basis_in, basis_out, query_in, query_out, lengths):
    in_width = basis_in.shape[0]
    mine = jnp.concatenate([query_in.T, query_out.T], axis=1)
    other = lax.ppermute(mine, "inp", ACROSS)
    pair = jnp.concatenate([mine, other], axis=0)
    groups = [(mine, other)]
    up = down = pair
    for _ in range(3):
        up, down = lax.ppermute(up, "inp", UP), lax.ppermute(down, "inp", DOWN)
        groups.append((up, down))
    groups.append((lax.ppermute(up[:RANK], "inp", UP), lax.ppermute(down[RANK:], "inp", DOWN)))
    keeps, gots = [], []
    for a, b in groups:
        keep, send = rotate(a, b, basis_in, basis_out)
        keeps.append(keep)
        gots.append(lax.ppermute(send, "out", CORES))
    codes = code(keeps, gots, in_width)
    codes = lax.all_to_all(codes, "out", 0, 0, tiled=True, axis_index_groups=CHIPS)
    codes = resum(codes, in_width)
    own = lax.all_to_all(codes, "out", 0, 0, tiled=True, axis_index_groups=CHIPS)
    sibling = lax.ppermute(own, "out", CORES)
    sides = project(own, sibling, acts, grads)
    sides = lax.all_to_all(sides, "inp", 0, 0, tiled=True)
    sums = score(lengths, sides)
    sums = lax.all_to_all(sums, "out", 0, 0, tiled=True)
    total = jnp.sum(sums[:, 0, : lengths.shape[0]], axis=0)
    return (total / lengths.astype(jnp.float32))[:, None]


def solution(mesh):
    placed = (
        P("out", "inp"),
        P("out", "inp"),
        P("inp", "out"),
        P("inp", "out"),
        P("out", "inp"),
        P("out", "inp"),
        P(),
    )
    return jax.shard_map(
        per_device, mesh=mesh, in_specs=placed, out_specs=P(None, "inp"), check_vma=False
    )
```

```python
import functools

import jax
import jax.numpy as jnp
from jax import lax
from jax.experimental import pallas as pl
from jax.experimental.pallas import tpu as pltpu
from jax.sharding import PartitionSpec as P

RANK = 32
LEVELS = 32700.0
STEPS = 64.0
PAD = 128
VMEM = pl.BlockSpec(memory_space=pltpu.VMEM)
SMEM = pl.BlockSpec(memory_space=pltpu.SMEM)
BRIEF = pl.CostEstimate(flops=100_000_000, bytes_accessed=100_000, transcendentals=0)


def params(mib):
    return pltpu.CompilerParams(vmem_limit_bytes=mib << 20)


def core_id():
    return lax.rem(lax.axis_index("out"), 2)


def level_of(x):
    largest = jnp.max(jnp.abs(x), axis=1, keepdims=True)
    return jnp.ceil(jnp.log2(jnp.maximum(largest, 1e-30)) * STEPS)


def encode(x, level):
    scaled = x * (jnp.exp2(level * (-1.0 / STEPS)) * LEVELS)
    scaled = jnp.clip(scaled, -32767.0, 32767.0)
    return jnp.round(scaled).astype(jnp.int32).astype(jnp.int16)


def unit_of(level):
    return jnp.exp2(level * (1.0 / STEPS)) * (1.0 / LEVELS)


def pack_levels(level_in, level_out):
    rows = level_in.shape[0]
    lane = lax.broadcasted_iota(jnp.int32, (rows, PAD), 1)
    both = jnp.where(lane < PAD // 2, level_in, level_out)
    return both.astype(jnp.int32).astype(jnp.int16)


def as_float(x):
    return x.astype(jnp.int32).astype(jnp.float32)


def units(tail):
    tail = as_float(tail)
    return unit_of(tail[:, 0:1]), unit_of(tail[:, PAD // 2 : PAD // 2 + 1])


def stage_kernel(basis_in, basis_out, out_in, out_out, sems):
    copies = [
        pltpu.make_async_copy(basis_in, out_in, sems.at[0]),
        pltpu.make_async_copy(basis_out, out_out, sems.at[1]),
    ]
    for copy in copies:
        copy.start()
    for copy in copies:
        copy.wait()


def stage(basis_in, basis_out):
    return pl.pallas_call(
        stage_kernel,
        in_specs=[pl.BlockSpec(memory_space=pltpu.HBM)] * 2,
        out_specs=[VMEM] * 2,
        out_shape=[pltpu.VMEM(x.shape, x.dtype) for x in (basis_in, basis_out)],
        scratch_shapes=[pltpu.SemaphoreType.DMA((2,))],
        compiler_params=params(16),
        cost_estimate=BRIEF,
    )(basis_in, basis_out)


def rotate_kernel(count, *refs):
    firsts, seconds = refs[:count], refs[count : 2 * count]
    basis_in, basis_out, keep, send, rows = refs[2 * count :]
    own = core_id() == 0
    half = keep.shape[0]
    lo = 0
    for first, second in zip(firsts, seconds):
        a, b = first[...], second[...]
        hi = lo + a.shape[0]
        rows[lo:hi] = jnp.where(own, a, b)
        rows[half + lo : half + hi] = jnp.where(own, b, a)
        lo = hi
    width = basis_in.shape[1]
    tile = 256
    for basis, base in ((basis_in, 0), (basis_out, width)):
        columns = slice(base, base + basis.shape[1])
        for lo in range(0, basis.shape[0], tile):
            got = lax.dot_general(
                rows[:, columns],
                basis[lo : lo + tile],
                (((1,), (1,)), ((), ())),
                preferred_element_type=jnp.float32,
            )
            keep[:, base + lo : base + lo + tile] = got[:half]
            send[:, base + lo : base + lo + tile] = got[half:]


def rotate(firsts, seconds, basis_in, basis_out):
    count = len(firsts)
    half, width = sum(x.shape[0] for x in firsts), firsts[0].shape[1]
    shape = jax.ShapeDtypeStruct((half, width), jnp.float32)
    return pl.pallas_call(
        functools.partial(rotate_kernel, count),
        in_specs=[VMEM] * (2 * count + 2),
        out_specs=[VMEM] * 2,
        out_shape=[shape, shape],
        scratch_shapes=[pltpu.VMEM((2 * half, width), jnp.bfloat16)],
        compiler_params=params(16),
        cost_estimate=pl.CostEstimate(
            flops=4 * half * (basis_in.size + basis_out.size),
            bytes_accessed=100_000,
            transcendentals=0,
        ),
    )(*firsts, *seconds, basis_in, basis_out)


def store_codes(total, in_width, store):
    side_in, side_out = total[:, :in_width], total[:, in_width:]
    level_in, level_out = level_of(side_in), level_of(side_out)
    store(0, in_width, encode(side_in, level_in))
    store(in_width, total.shape[1], encode(side_out, level_out))
    store(total.shape[1], total.shape[1] + PAD, pack_levels(level_in, level_out))


def code_kernel(in_width, keep, got, *refs):
    done, out = refs[:-1], refs[-1]
    slot = 0
    for codes in done:
        out[slot : slot + codes.shape[0]] = codes[...]
        slot += codes.shape[0]
    for part in range(keep.shape[0] // RANK):
        rows = slice(part * RANK, (part + 1) * RANK)

        def store(lo, hi, value, slot=slot + part):
            out[slot, :, lo:hi] = value

        store_codes(keep[rows] + got[rows], in_width, store)


def code(keep, got, in_width, *done):
    slots = keep.shape[0] // RANK + sum(codes.shape[0] for codes in done)
    return pl.pallas_call(
        functools.partial(code_kernel, in_width),
        in_specs=[VMEM] * (2 + len(done)),
        out_specs=VMEM,
        out_shape=jax.ShapeDtypeStruct((slots, RANK, keep.shape[1] + PAD), jnp.int16),
        compiler_params=params(16),
        cost_estimate=BRIEF,
    )(keep, got, *done)


def resum_kernel(in_width, codes, out):
    width = codes.shape[2] - PAD
    total_in = total_out = 0.0
    for source in range(codes.shape[0]):
        unit_in, unit_out = units(codes[source, :, width:])
        total_in += as_float(codes[source, :, :in_width]) * unit_in
        total_out += as_float(codes[source, :, in_width:width]) * unit_out

    def store(lo, hi, value):
        for target in range(out.shape[0]):
            out[target, :, lo:hi] = value

    store_codes(jnp.concatenate([total_in, total_out], axis=1), in_width, store)


def resum(codes, in_width):
    return pl.pallas_call(
        functools.partial(resum_kernel, in_width),
        in_specs=[VMEM],
        out_specs=VMEM,
        out_shape=jax.ShapeDtypeStruct(codes.shape, jnp.int16),
        compiler_params=params(24),
    )(codes)


def project_kernel(own, other, acts, grads, out):
    core = core_id()
    place = lax.axis_index("inp")
    x_lo, z = place // 8, lax.rem(place, 8)
    in_width, tokens = acts.shape[1], acts.shape[0]
    width = own.shape[2] - PAD
    contract = (((1,), (1,)), ((), ()))

    def side(codes, unit, data):
        value = as_float(codes)
        high = value.astype(jnp.bfloat16)
        low = (value - high.astype(jnp.float32)).astype(jnp.bfloat16)
        data = data[...]
        got = lax.dot_general(high, data, contract, preferred_element_type=jnp.float32)
        got += lax.dot_general(low, data, contract, preferred_element_type=jnp.float32)
        return got * unit

    for codes, half in ((own, core), (other, 1 - core)):
        rows = codes.shape[0] * RANK
        unit_in, unit_out = units(codes[:, :, width:].reshape(rows, PAD))
        side_in = side(codes[:, :, :in_width].reshape(rows, in_width), unit_in, acts)
        side_out = side(codes[:, :, in_width:width].reshape(rows, width - in_width), unit_out, grads)
        level_in, level_out = level_of(side_in), level_of(side_out)
        code_in, code_out = encode(side_in, level_in), encode(side_out, level_out)
        tail = pack_levels(level_in, level_out)
        sign = 2 * half - 1
        for slot in range(8):
            away = (slot + 1) // 2
            cross = (slot + 1) % 2 if 0 < slot < 7 else half
            target = lax.rem(x_lo + cross, 2) * 8 + lax.rem(z + sign * away + 8, 8)
            span = slice(slot * RANK, (slot + 1) * RANK)
            out[target, :, 0:tokens] = code_in[span]
            out[target, :, tokens : 2 * tokens] = code_out[span]
            out[target, :, 2 * tokens :] = tail[span]


def project(own, other, acts, grads):
    tokens = acts.shape[0]
    return pl.pallas_call(
        project_kernel,
        in_specs=[VMEM] * 4,
        out_specs=VMEM,
        out_shape=jax.ShapeDtypeStruct((16, RANK, 2 * tokens + PAD), jnp.int16),
        compiler_params=params(40),
    )(own, other, acts, grads)


def score_kernel(lengths, codes, out):
    tokens = (codes.shape[2] - PAD) // 2
    side_in = side_out = 0.0
    for source in range(codes.shape[0]):
        unit_in, unit_out = units(codes[source, :, 2 * tokens :])
        side_in += as_float(codes[source, :, :tokens]) * unit_in
        side_out += as_float(codes[source, :, tokens : 2 * tokens]) * unit_out
    per_token = jnp.sum(side_in * side_out, axis=0, keepdims=True)
    position = lax.axis_index("out") * tokens + lax.broadcasted_iota(jnp.int32, (1, tokens), 1)
    lane = lax.broadcasted_iota(jnp.int32, (1, 128), 1)
    sums = jnp.zeros((1, 128), jnp.float32)
    start = jnp.int32(0)
    for example in range(lengths.shape[0]):
        finish = start + lengths[example]
        inside = (position >= start) & (position < finish)
        total = jnp.sum(jnp.where(inside, per_token, 0.0), axis=1, keepdims=True)
        sums = jnp.where(lane == example, total, sums)
        start = finish
    for target in range(out.shape[0]):
        out[target] = jnp.broadcast_to(sums, out.shape[1:])


def score(lengths, codes):
    return pl.pallas_call(
        score_kernel,
        in_specs=[SMEM, VMEM],
        out_specs=VMEM,
        out_shape=jax.ShapeDtypeStruct((16, 8, 128), jnp.float32),
        compiler_params=params(16),
    )(lengths, codes)


UP = [(x * 8 + z, x * 8 + (z + 1) % 8) for x in range(2) for z in range(8)]
DOWN = [(b, a) for a, b in UP]
ACROSS = [(i, (i + 8) % 16) for i in range(16)]
CORES = [(i, i ^ 1) for i in range(16)]
CHIPS = [[2 * chip + core for chip in range(8)] for core in range(2)]


def per_device(acts, grads, basis_in, basis_out, query_in, query_out, lengths):
    in_width = basis_in.shape[0]
    mine = jnp.concatenate([query_in.T, query_out.T], axis=1)
    other = lax.ppermute(mine, "inp", ACROSS)
    other, basis_in, basis_out = lax.optimization_barrier(
        (other, *stage(basis_in, basis_out))
    )
    basis_in = pltpu.with_memory_space_constraint(basis_in, pltpu.VMEM)
    basis_out = pltpu.with_memory_space_constraint(basis_out, pltpu.VMEM)


    def hop(ends):
        up, down = ends
        return lax.ppermute(up, "inp", UP), lax.ppermute(down, "inp", DOWN)

    def rotated(*ends):
        firsts, seconds = zip(*ends)
        return rotate(firsts, seconds, basis_in, basis_out)

    def finish(rotated, *done):
        keep, send = rotated
        return code(keep, lax.ppermute(send, "out", CORES), in_width, *done)

    a1 = hop((mine, mine))
    b1 = hop((other, other))
    a2 = hop(a1)
    b2 = hop(b1)
    a3 = hop(a2)
    b3 = hop(b2)
    a4 = lax.ppermute(a3[0], "inp", UP)
    b4 = lax.ppermute(b3[1], "inp", DOWN)
    keep, send = rotated((mine, other), a1, b1, a2, b2, a3, b3)
    send, a4, b4 = lax.optimization_barrier((send, a4, b4))
    end = rotated((a4, b4))
    codes = finish(end, finish((keep, send)))
    codes = lax.all_to_all(codes, "out", 0, 0, tiled=True, axis_index_groups=CHIPS)
    codes = resum(codes, in_width)
    own = lax.all_to_all(codes, "out", 0, 0, tiled=True, axis_index_groups=CHIPS)
    sibling = lax.ppermute(own, "out", CORES)
    sides = project(own, sibling, acts, grads)
    sides = lax.all_to_all(sides, "inp", 0, 0, tiled=True)
    sums = score(lengths, sides)
    sums = lax.all_to_all(sums, "out", 0, 0, tiled=True)
    total = jnp.sum(sums[:, 0, : lengths.shape[0]], axis=0)
    return (total / lengths.astype(jnp.float32))[:, None]


def solution(mesh):
    placed = (
        P("out", "inp"),
        P("out", "inp"),
        P("inp", "out"),
        P("inp", "out"),
        P("out", "inp"),
        P("out", "inp"),
        P(),
    )
    return jax.shard_map(
        per_device, mesh=mesh, in_specs=placed, out_specs=P(None, "inp"), check_vma=False
    )
```

```python
import functools

import jax
import jax.numpy as jnp
from jax import lax
from jax.experimental import pallas as pl
from jax.experimental.pallas import tpu as pltpu
from jax.sharding import PartitionSpec as P

RANK = 32
LEVELS = 32700.0
STEPS = 64.0
PAD = 128
VMEM = pl.BlockSpec(memory_space=pltpu.VMEM)
SMEM = pl.BlockSpec(memory_space=pltpu.SMEM)
BRIEF = pl.CostEstimate(flops=100_000_000, bytes_accessed=100_000, transcendentals=0)


def params(mib):
    return pltpu.CompilerParams(vmem_limit_bytes=mib << 20)


def core_id():
    return lax.rem(lax.axis_index("out"), 2)


def level_of(x):
    largest = jnp.max(jnp.abs(x), axis=1, keepdims=True)
    return jnp.ceil(jnp.log2(jnp.maximum(largest, 1e-30)) * STEPS)


def encode(x, level):
    scaled = x * (jnp.exp2(level * (-1.0 / STEPS)) * LEVELS)
    scaled = jnp.clip(scaled, -32767.0, 32767.0)
    return jnp.round(scaled).astype(jnp.int32).astype(jnp.int16)


def unit_of(level):
    return jnp.exp2(level * (1.0 / STEPS)) * (1.0 / LEVELS)


def pack_levels(level_in, level_out):
    rows = level_in.shape[0]
    lane = lax.broadcasted_iota(jnp.int32, (rows, PAD), 1)
    both = jnp.where(lane < PAD // 2, level_in, level_out)
    return both.astype(jnp.int32).astype(jnp.int16)


def as_float(x):
    return x.astype(jnp.int32).astype(jnp.float32)


def units(tail):
    tail = as_float(tail)
    return unit_of(tail[:, 0:1]), unit_of(tail[:, PAD // 2 : PAD // 2 + 1])


def stage_kernel(basis_in, basis_out, out_in, out_out, sems):
    copies = [
        pltpu.make_async_copy(basis_in, out_in, sems.at[0]),
        pltpu.make_async_copy(basis_out, out_out, sems.at[1]),
    ]
    for copy in copies:
        copy.start()
    for copy in copies:
        copy.wait()


def stage(basis_in, basis_out):
    return pl.pallas_call(
        stage_kernel,
        in_specs=[pl.BlockSpec(memory_space=pltpu.HBM)] * 2,
        out_specs=[VMEM] * 2,
        out_shape=[pltpu.VMEM(x.shape, x.dtype) for x in (basis_in, basis_out)],
        scratch_shapes=[pltpu.SemaphoreType.DMA((2,))],
        compiler_params=params(16),
        cost_estimate=BRIEF,
    )(*[pltpu.with_memory_space_constraint(x, pltpu.HBM) for x in (basis_in, basis_out)])


def rotate_kernel(count, *refs):
    firsts, seconds = refs[:count], refs[count : 2 * count]
    basis_in, basis_out, keep, send, rows = refs[2 * count :]
    own = core_id() == 0
    half = keep.shape[0]
    lo = 0
    for first, second in zip(firsts, seconds):
        a, b = first[...], second[...]
        hi = lo + a.shape[0]
        rows[lo:hi] = jnp.where(own, a, b)
        rows[half + lo : half + hi] = jnp.where(own, b, a)
        lo = hi
    width = basis_in.shape[1]
    tile = 256
    for basis, base in ((basis_in, 0), (basis_out, width)):
        columns = slice(base, base + basis.shape[1])
        for lo in range(0, basis.shape[0], tile):
            got = lax.dot_general(
                rows[:, columns],
                basis[lo : lo + tile],
                (((1,), (1,)), ((), ())),
                preferred_element_type=jnp.float32,
            )
            keep[:, base + lo : base + lo + tile] = got[:half]
            send[:, base + lo : base + lo + tile] = got[half:]


def rotate(firsts, seconds, basis_in, basis_out):
    count = len(firsts)
    half, width = sum(x.shape[0] for x in firsts), firsts[0].shape[1]
    shape = jax.ShapeDtypeStruct((half, width), jnp.float32)
    return pl.pallas_call(
        functools.partial(rotate_kernel, count),
        in_specs=[VMEM] * (2 * count + 2),
        out_specs=[VMEM] * 2,
        out_shape=[shape, shape],
        scratch_shapes=[pltpu.VMEM((2 * half, width), jnp.bfloat16)],
        compiler_params=params(16),
        cost_estimate=pl.CostEstimate(
            flops=4 * half * (basis_in.size + basis_out.size),
            bytes_accessed=100_000,
            transcendentals=0,
        ),
    )(*firsts, *seconds, basis_in, basis_out)


def store_codes(total, in_width, store):
    side_in, side_out = total[:, :in_width], total[:, in_width:]
    level_in, level_out = level_of(side_in), level_of(side_out)
    store(0, in_width, encode(side_in, level_in))
    store(in_width, total.shape[1], encode(side_out, level_out))
    store(total.shape[1], total.shape[1] + PAD, pack_levels(level_in, level_out))


def code_kernel(in_width, keep, got, *refs):
    done, out = refs[:-1], refs[-1]
    slot = 0
    for codes in done:
        out[slot : slot + codes.shape[0]] = codes[...]
        slot += codes.shape[0]
    for part in range(keep.shape[0] // RANK):
        rows = slice(part * RANK, (part + 1) * RANK)

        def store(lo, hi, value, slot=slot + part):
            out[slot, :, lo:hi] = value

        store_codes(keep[rows] + got[rows], in_width, store)


def code(keep, got, in_width, *done):
    slots = keep.shape[0] // RANK + sum(codes.shape[0] for codes in done)
    return pl.pallas_call(
        functools.partial(code_kernel, in_width),
        in_specs=[VMEM] * (2 + len(done)),
        out_specs=VMEM,
        out_shape=jax.ShapeDtypeStruct((slots, RANK, keep.shape[1] + PAD), jnp.int16),
        compiler_params=params(16),
        cost_estimate=BRIEF,
    )(keep, got, *done)


def resum_kernel(in_width, codes, out):
    width = codes.shape[2] - PAD
    total_in = total_out = 0.0
    for source in range(codes.shape[0]):
        unit_in, unit_out = units(codes[source, :, width:])
        total_in += as_float(codes[source, :, :in_width]) * unit_in
        total_out += as_float(codes[source, :, in_width:width]) * unit_out

    def store(lo, hi, value):
        for target in range(out.shape[0]):
            out[target, :, lo:hi] = value

    store_codes(jnp.concatenate([total_in, total_out], axis=1), in_width, store)


def resum(codes, in_width):
    return pl.pallas_call(
        functools.partial(resum_kernel, in_width),
        in_specs=[VMEM],
        out_specs=VMEM,
        out_shape=jax.ShapeDtypeStruct(codes.shape, jnp.int16),
        compiler_params=params(24),
    )(codes)


def project_kernel(is_own, *refs):
    codes, acts, grads, out = refs[0], refs[1], refs[2], refs[-1]
    half = core_id() if is_own else 1 - core_id()
    place = lax.axis_index("inp")
    x_lo, z = place // 8, lax.rem(place, 8)
    in_width, tokens = acts.shape[1], acts.shape[0]
    width = codes.shape[2] - PAD
    contract = (((1,), (1,)), ((), ()))

    def side(codes, unit, data):
        value = as_float(codes)
        high = value.astype(jnp.bfloat16)
        low = (value - high.astype(jnp.float32)).astype(jnp.bfloat16)
        data = data[...]
        got = lax.dot_general(high, data, contract, preferred_element_type=jnp.float32)
        got += lax.dot_general(low, data, contract, preferred_element_type=jnp.float32)
        return got * unit

    rows = codes.shape[0] * RANK
    unit_in, unit_out = units(codes[:, :, width:].reshape(rows, PAD))
    side_in = side(codes[:, :, :in_width].reshape(rows, in_width), unit_in, acts)
    side_out = side(codes[:, :, in_width:width].reshape(rows, width - in_width), unit_out, grads)
    level_in, level_out = level_of(side_in), level_of(side_out)
    code_in, code_out = encode(side_in, level_in), encode(side_out, level_out)
    tail = pack_levels(level_in, level_out)
    sign = 2 * half - 1
    for slot in range(8):
        away = (slot + 1) // 2
        cross = (slot + 1) % 2 if 0 < slot < 7 else half
        target = lax.rem(x_lo + cross, 2) * 8 + lax.rem(z + sign * away + 8, 8)
        span = slice(slot * RANK, (slot + 1) * RANK)
        out[target, :, 0:tokens] = code_in[span]
        out[target, :, tokens : 2 * tokens] = code_out[span]
        out[target, :, 2 * tokens :] = tail[span]


def project(codes, acts, grads, *filled):
    tokens = acts.shape[0]
    return pl.pallas_call(
        functools.partial(project_kernel, not filled),
        in_specs=[VMEM] * (3 + len(filled)),
        out_specs=VMEM,
        out_shape=jax.ShapeDtypeStruct((16, RANK, 2 * tokens + PAD), jnp.int16),
        input_output_aliases={3: 0} if filled else {},
        compiler_params=params(40),
        cost_estimate=BRIEF,
    )(codes, acts, grads, *filled)


def score_kernel(lengths, codes, out):
    tokens = (codes.shape[2] - PAD) // 2
    side_in = side_out = 0.0
    for source in range(codes.shape[0]):
        unit_in, unit_out = units(codes[source, :, 2 * tokens :])
        side_in += as_float(codes[source, :, :tokens]) * unit_in
        side_out += as_float(codes[source, :, tokens : 2 * tokens]) * unit_out
    per_token = jnp.sum(side_in * side_out, axis=0, keepdims=True)
    position = lax.axis_index("out") * tokens + lax.broadcasted_iota(jnp.int32, (1, tokens), 1)
    lane = lax.broadcasted_iota(jnp.int32, (1, 128), 1)
    sums = jnp.zeros((1, 128), jnp.float32)
    start = jnp.int32(0)
    for example in range(lengths.shape[0]):
        finish = start + lengths[example]
        inside = (position >= start) & (position < finish)
        total = jnp.sum(jnp.where(inside, per_token, 0.0), axis=1, keepdims=True)
        sums = jnp.where(lane == example, total, sums)
        start = finish
    for target in range(out.shape[0]):
        out[target] = jnp.broadcast_to(sums, out.shape[1:])


def score(lengths, codes):
    return pl.pallas_call(
        score_kernel,
        in_specs=[SMEM, VMEM],
        out_specs=VMEM,
        out_shape=jax.ShapeDtypeStruct((16, 8, 128), jnp.float32),
        compiler_params=params(16),
    )(lengths, codes)


UP = [(x * 8 + z, x * 8 + (z + 1) % 8) for x in range(2) for z in range(8)]
DOWN = [(b, a) for a, b in UP]
ACROSS = [(i, (i + 8) % 16) for i in range(16)]
CORES = [(i, i ^ 1) for i in range(16)]
CHIPS = [[2 * chip + core for chip in range(8)] for core in range(2)]


def per_device(acts, grads, basis_in, basis_out, query_in, query_out, lengths):
    in_width = basis_in.shape[0]
    mine = jnp.concatenate([query_in.T, query_out.T], axis=1)
    other = lax.ppermute(mine, "inp", ACROSS)
    other, basis_in, basis_out = lax.optimization_barrier(
        (other, *stage(basis_in, basis_out))
    )
    basis_in = pltpu.with_memory_space_constraint(basis_in, pltpu.VMEM)
    basis_out = pltpu.with_memory_space_constraint(basis_out, pltpu.VMEM)


    def hop(ends):
        up, down = ends
        return lax.ppermute(up, "inp", UP), lax.ppermute(down, "inp", DOWN)

    def rotated(*ends):
        firsts, seconds = zip(*ends)
        return rotate(firsts, seconds, basis_in, basis_out)

    def finish(rotated, *done):
        keep, send = rotated
        return code(keep, lax.ppermute(send, "out", CORES), in_width, *done)

    a1 = hop((mine, mine))
    b1 = hop((other, other))
    a2 = hop(a1)
    b2 = hop(b1)
    a3 = hop(a2)
    b3 = hop(b2)
    a4 = lax.ppermute(a3[0], "inp", UP)
    b4 = lax.ppermute(b3[1], "inp", DOWN)
    keep, send = rotated((mine, other), a1, b1, a2, b2, a3, b3)
    send, a4, b4 = lax.optimization_barrier((send, a4, b4))
    end = rotated((a4, b4))
    codes = finish(end, finish((keep, send)))
    codes = lax.all_to_all(codes, "out", 0, 0, tiled=True, axis_index_groups=CHIPS)
    codes = resum(codes, in_width)
    own = lax.all_to_all(codes, "out", 0, 0, tiled=True, axis_index_groups=CHIPS)
    sibling = lax.ppermute(own, "out", CORES)
    sides = project(sibling, acts, grads, project(own, acts, grads))
    sides = lax.all_to_all(sides, "inp", 0, 0, tiled=True)
    sums = score(lengths, sides)
    sums = lax.all_to_all(sums, "out", 0, 0, tiled=True)
    total = jnp.sum(sums[:, 0, : lengths.shape[0]], axis=0)
    return (total / lengths.astype(jnp.float32))[:, None]


def solution(mesh):
    placed = (
        P("out", "inp"),
        P("out", "inp"),
        P("inp", "out"),
        P("inp", "out"),
        P("out", "inp"),
        P("out", "inp"),
        P(),
    )
    return jax.shard_map(
        per_device, mesh=mesh, in_specs=placed, out_specs=P(None, "inp"), check_vma=False
    )
```

```python
import functools

import jax
import jax.numpy as jnp
from jax import lax
from jax.experimental import pallas as pl
from jax.experimental.pallas import tpu as pltpu
from jax.sharding import PartitionSpec as P

RANK = 32
LEVELS = 32700.0
STEPS = 64.0
PAD = 128
VMEM = pl.BlockSpec(memory_space=pltpu.VMEM)
SMEM = pl.BlockSpec(memory_space=pltpu.SMEM)
BRIEF = pl.CostEstimate(flops=100_000_000, bytes_accessed=100_000, transcendentals=0)


def params(mib):
    return pltpu.CompilerParams(vmem_limit_bytes=mib << 20)


def core_id():
    return lax.rem(lax.axis_index("out"), 2)


def level_of(x):
    largest = jnp.max(jnp.abs(x), axis=1, keepdims=True)
    return jnp.ceil(jnp.log2(jnp.maximum(largest, 1e-30)) * STEPS)


def encode(x, level):
    scaled = x * (jnp.exp2(level * (-1.0 / STEPS)) * LEVELS)
    scaled = jnp.clip(scaled, -32767.0, 32767.0)
    return jnp.round(scaled).astype(jnp.int32).astype(jnp.int16)


def unit_of(level):
    return jnp.exp2(level * (1.0 / STEPS)) * (1.0 / LEVELS)


def pack_levels(level_in, level_out):
    rows = level_in.shape[0]
    lane = lax.broadcasted_iota(jnp.int32, (rows, PAD), 1)
    both = jnp.where(lane < PAD // 2, level_in, level_out)
    return both.astype(jnp.int32).astype(jnp.int16)


def as_float(x):
    return x.astype(jnp.int32).astype(jnp.float32)


def units(tail):
    tail = as_float(tail)
    return unit_of(tail[:, 0:1]), unit_of(tail[:, PAD // 2 : PAD // 2 + 1])


def stage_kernel(basis_in, basis_out, out_in, out_out, sems):
    copies = [
        pltpu.make_async_copy(basis_in, out_in, sems.at[0]),
        pltpu.make_async_copy(basis_out, out_out, sems.at[1]),
    ]
    for copy in copies:
        copy.start()
    for copy in copies:
        copy.wait()


def stage(basis_in, basis_out):
    return pl.pallas_call(
        stage_kernel,
        in_specs=[pl.BlockSpec(memory_space=pltpu.HBM)] * 2,
        out_specs=[VMEM] * 2,
        out_shape=[pltpu.VMEM(x.shape, x.dtype) for x in (basis_in, basis_out)],
        scratch_shapes=[pltpu.SemaphoreType.DMA((2,))],
        compiler_params=params(16),
        cost_estimate=BRIEF,
    )(*[pltpu.with_memory_space_constraint(x, pltpu.HBM) for x in (basis_in, basis_out)])


def rotate_kernel(count, *refs):
    firsts, seconds = refs[:count], refs[count : 2 * count]
    basis_in, basis_out, keep, send, rows = refs[2 * count :]
    own = core_id() == 0
    half = keep.shape[0]
    lo = 0
    for first, second in zip(firsts, seconds):
        a, b = first[...], second[...]
        hi = lo + a.shape[0]
        rows[lo:hi] = jnp.where(own, a, b)
        rows[half + lo : half + hi] = jnp.where(own, b, a)
        lo = hi
    width = basis_in.shape[1]
    tile = 256
    for basis, base in ((basis_in, 0), (basis_out, width)):
        columns = slice(base, base + basis.shape[1])
        for lo in range(0, basis.shape[0], tile):
            got = lax.dot_general(
                rows[:, columns],
                basis[lo : lo + tile],
                (((1,), (1,)), ((), ())),
                preferred_element_type=jnp.float32,
            )
            keep[:, base + lo : base + lo + tile] = got[:half]
            send[:, base + lo : base + lo + tile] = got[half:]


def rotate(firsts, seconds, basis_in, basis_out):
    count = len(firsts)
    half, width = sum(x.shape[0] for x in firsts), firsts[0].shape[1]
    shape = jax.ShapeDtypeStruct((half, width), jnp.float32)
    return pl.pallas_call(
        functools.partial(rotate_kernel, count),
        in_specs=[VMEM] * (2 * count + 2),
        out_specs=[VMEM] * 2,
        out_shape=[shape, shape],
        scratch_shapes=[pltpu.VMEM((2 * half, width), jnp.bfloat16)],
        compiler_params=params(16),
        cost_estimate=pl.CostEstimate(
            flops=4 * half * (basis_in.size + basis_out.size),
            bytes_accessed=100_000,
            transcendentals=0,
        ),
    )(*firsts, *seconds, basis_in, basis_out)


def store_codes(total, in_width, store):
    side_in, side_out = total[:, :in_width], total[:, in_width:]
    level_in, level_out = level_of(side_in), level_of(side_out)
    store(0, in_width, encode(side_in, level_in))
    store(in_width, total.shape[1], encode(side_out, level_out))
    store(total.shape[1], total.shape[1] + PAD, pack_levels(level_in, level_out))


def code_kernel(in_width, keep, got, *refs):
    done, out = refs[:-1], refs[-1]
    slot = 0
    for codes in done:
        out[slot : slot + codes.shape[0]] = codes[...]
        slot += codes.shape[0]
    for part in range(keep.shape[0] // RANK):
        rows = slice(part * RANK, (part + 1) * RANK)

        def store(lo, hi, value, slot=slot + part):
            out[slot, :, lo:hi] = value

        store_codes(keep[rows] + got[rows], in_width, store)


def code(keep, got, in_width, *done):
    slots = keep.shape[0] // RANK + sum(codes.shape[0] for codes in done)
    return pl.pallas_call(
        functools.partial(code_kernel, in_width),
        in_specs=[VMEM] * (2 + len(done)),
        out_specs=VMEM,
        out_shape=jax.ShapeDtypeStruct((slots, RANK, keep.shape[1] + PAD), jnp.int16),
        compiler_params=params(16),
        cost_estimate=BRIEF,
    )(keep, got, *done)


def resum_kernel(in_width, codes, out):
    width = codes.shape[2] - PAD
    total_in = total_out = 0.0
    for source in range(codes.shape[0]):
        unit_in, unit_out = units(codes[source, :, width:])
        total_in += as_float(codes[source, :, :in_width]) * unit_in
        total_out += as_float(codes[source, :, in_width:width]) * unit_out

    def store(lo, hi, value):
        for target in range(out.shape[0]):
            out[target, :, lo:hi] = value

    store_codes(jnp.concatenate([total_in, total_out], axis=1), in_width, store)


def resum(codes, in_width):
    return pl.pallas_call(
        functools.partial(resum_kernel, in_width),
        in_specs=[VMEM],
        out_specs=VMEM,
        out_shape=jax.ShapeDtypeStruct(codes.shape, jnp.int16),
        compiler_params=params(24),
    )(codes)


def project_kernel(is_own, *refs):
    codes, acts, grads, out = refs[0], refs[1], refs[2], refs[-1]
    half = core_id() if is_own else 1 - core_id()
    place = lax.axis_index("inp")
    x_lo, z = place // 8, lax.rem(place, 8)
    in_width, tokens = acts.shape[1], acts.shape[0]
    width = codes.shape[2] - PAD
    contract = (((1,), (1,)), ((), ()))

    def side(codes, unit, data):
        value = as_float(codes)
        high = value.astype(jnp.bfloat16)
        low = (value - high.astype(jnp.float32)).astype(jnp.bfloat16)
        data = data[...]
        got = lax.dot_general(high, data, contract, preferred_element_type=jnp.float32)
        got += lax.dot_general(low, data, contract, preferred_element_type=jnp.float32)
        return got * unit

    rows = codes.shape[0] * RANK
    unit_in, unit_out = units(codes[:, :, width:].reshape(rows, PAD))
    side_in = side(codes[:, :, :in_width].reshape(rows, in_width), unit_in, acts)
    side_out = side(codes[:, :, in_width:width].reshape(rows, width - in_width), unit_out, grads)
    level_in, level_out = level_of(side_in), level_of(side_out)
    code_in, code_out = encode(side_in, level_in), encode(side_out, level_out)
    tail = pack_levels(level_in, level_out)
    sign = 2 * half - 1
    for slot in range(8):
        away = (slot + 1) // 2
        cross = (slot + 1) % 2 if 0 < slot < 7 else half
        target = lax.rem(x_lo + cross, 2) * 8 + lax.rem(z + sign * away + 8, 8)
        span = slice(slot * RANK, (slot + 1) * RANK)
        out[target, :, 0:tokens] = code_in[span]
        out[target, :, tokens : 2 * tokens] = code_out[span]
        out[target, :, 2 * tokens :] = tail[span]


def project(codes, acts, grads, *filled):
    tokens = acts.shape[0]
    return pl.pallas_call(
        functools.partial(project_kernel, not filled),
        in_specs=[VMEM] * (3 + len(filled)),
        out_specs=VMEM,
        out_shape=jax.ShapeDtypeStruct((16, RANK, 2 * tokens + PAD), jnp.int16),
        input_output_aliases={3: 0} if filled else {},
        compiler_params=params(40),
        cost_estimate=BRIEF,
    )(codes, acts, grads, *filled)


def score_kernel(lengths, codes, out):
    tokens = (codes.shape[2] - PAD) // 2
    side_in = side_out = 0.0
    for source in range(codes.shape[0]):
        unit_in, unit_out = units(codes[source, :, 2 * tokens :])
        side_in += as_float(codes[source, :, :tokens]) * unit_in
        side_out += as_float(codes[source, :, tokens : 2 * tokens]) * unit_out
    per_token = jnp.sum(side_in * side_out, axis=0, keepdims=True)
    position = lax.axis_index("out") * tokens + lax.broadcasted_iota(jnp.int32, (1, tokens), 1)
    lane = lax.broadcasted_iota(jnp.int32, (1, 128), 1)
    sums = jnp.zeros((1, 128), jnp.float32)
    start = jnp.int32(0)
    for example in range(lengths.shape[0]):
        finish = start + lengths[example]
        inside = (position >= start) & (position < finish)
        total = jnp.sum(jnp.where(inside, per_token, 0.0), axis=1, keepdims=True)
        sums = jnp.where(lane == example, total, sums)
        start = finish
    for target in range(out.shape[0]):
        out[target] = jnp.broadcast_to(sums, out.shape[1:])


def score(lengths, codes):
    return pl.pallas_call(
        score_kernel,
        in_specs=[SMEM, VMEM],
        out_specs=VMEM,
        out_shape=jax.ShapeDtypeStruct((16, 8, 128), jnp.float32),
        compiler_params=params(16),
    )(lengths, codes)


UP = [(x * 8 + z, x * 8 + (z + 1) % 8) for x in range(2) for z in range(8)]
DOWN = [(b, a) for a, b in UP]
ACROSS = [(i, (i + 8) % 16) for i in range(16)]
CORES = [(i, i ^ 1) for i in range(16)]
CHIPS = [[2 * chip + core for chip in range(8)] for core in range(2)]


def per_device(acts, grads, basis_in, basis_out, query_in, query_out, lengths):
    in_width = basis_in.shape[0]
    mine = jnp.concatenate([query_in.T, query_out.T], axis=1)
    other = lax.ppermute(mine, "inp", ACROSS)


    def hop(ends):
        up, down = ends
        return lax.ppermute(up, "inp", UP), lax.ppermute(down, "inp", DOWN)

    def rotated(*ends):
        firsts, seconds = zip(*ends)
        return rotate(firsts, seconds, basis_in, basis_out)

    def finish(rotated, *done):
        keep, send = rotated
        return code(keep, lax.ppermute(send, "out", CORES), in_width, *done)

    a1 = hop((mine, mine))
    b1 = hop((other, other))
    a2 = hop(a1)
    a2, basis_in, basis_out = lax.optimization_barrier(
        (a2, *stage(basis_in, basis_out))
    )
    basis_in = pltpu.with_memory_space_constraint(basis_in, pltpu.VMEM)
    basis_out = pltpu.with_memory_space_constraint(basis_out, pltpu.VMEM)
    b2 = hop(b1)
    a3 = hop(a2)
    b3 = hop(b2)
    a4 = lax.ppermute(a3[0], "inp", UP)
    b4 = lax.ppermute(b3[1], "inp", DOWN)
    keep, send = rotated((mine, other), a1, b1, a2, b2, a3, b3)
    send, a4, b4 = lax.optimization_barrier((send, a4, b4))
    end = rotated((a4, b4))
    codes = finish(end, finish((keep, send)))
    codes = lax.all_to_all(codes, "out", 0, 0, tiled=True, axis_index_groups=CHIPS)
    codes = resum(codes, in_width)
    own = lax.all_to_all(codes, "out", 0, 0, tiled=True, axis_index_groups=CHIPS)
    sibling = lax.ppermute(own, "out", CORES)
    sides = project(sibling, acts, grads, project(own, acts, grads))
    sides = lax.all_to_all(sides, "inp", 0, 0, tiled=True)
    sums = score(lengths, sides)
    sums = lax.all_to_all(sums, "out", 0, 0, tiled=True)
    total = jnp.sum(sums[:, 0, : lengths.shape[0]], axis=0)
    return (total / lengths.astype(jnp.float32))[:, None]


def solution(mesh):
    placed = (
        P("out", "inp"),
        P("out", "inp"),
        P("inp", "out"),
        P("inp", "out"),
        P("out", "inp"),
        P("out", "inp"),
        P(),
    )
    return jax.shard_map(
        per_device, mesh=mesh, in_specs=placed, out_specs=P(None, "inp"), check_vma=False
    )
```

```python
import functools

import jax
import jax.numpy as jnp
from jax import lax
from jax.experimental import pallas as pl
from jax.experimental.pallas import tpu as pltpu
from jax.sharding import PartitionSpec as P

RANK = 32
LEVELS = 32700.0
STEPS = 64.0
PAD = 128
VMEM = pl.BlockSpec(memory_space=pltpu.VMEM)
SMEM = pl.BlockSpec(memory_space=pltpu.SMEM)
BRIEF = pl.CostEstimate(flops=100_000_000, bytes_accessed=100_000, transcendentals=0)


def params(mib):
    return pltpu.CompilerParams(vmem_limit_bytes=mib << 20)


def core_id():
    return lax.rem(lax.axis_index("out"), 2)


def level_of(x):
    largest = jnp.max(jnp.abs(x), axis=1, keepdims=True)
    return jnp.ceil(jnp.log2(jnp.maximum(largest, 1e-30)) * STEPS)


def encode(x, level):
    scaled = x * (jnp.exp2(level * (-1.0 / STEPS)) * LEVELS)
    scaled = jnp.clip(scaled, -32767.0, 32767.0)
    return jnp.round(scaled).astype(jnp.int32).astype(jnp.int16)


def unit_of(level):
    return jnp.exp2(level * (1.0 / STEPS)) * (1.0 / LEVELS)


def pack_levels(level_in, level_out):
    rows = level_in.shape[0]
    lane = lax.broadcasted_iota(jnp.int32, (rows, PAD), 1)
    both = jnp.where(lane < PAD // 2, level_in, level_out)
    return both.astype(jnp.int32).astype(jnp.int16)


def as_float(x):
    return x.astype(jnp.int32).astype(jnp.float32)


def units(tail):
    tail = as_float(tail)
    return unit_of(tail[:, 0:1]), unit_of(tail[:, PAD // 2 : PAD // 2 + 1])


def stage_kernel(basis_in, basis_out, out_in, out_out, sems):
    copies = [
        pltpu.make_async_copy(basis_in, out_in, sems.at[0]),
        pltpu.make_async_copy(basis_out, out_out, sems.at[1]),
    ]
    for copy in copies:
        copy.start()
    for copy in copies:
        copy.wait()


def stage(basis_in, basis_out):
    return pl.pallas_call(
        stage_kernel,
        in_specs=[pl.BlockSpec(memory_space=pltpu.HBM)] * 2,
        out_specs=[VMEM] * 2,
        out_shape=[pltpu.VMEM(x.shape, x.dtype) for x in (basis_in, basis_out)],
        scratch_shapes=[pltpu.SemaphoreType.DMA((2,))],
        compiler_params=params(16),
        cost_estimate=BRIEF,
    )(*[pltpu.with_memory_space_constraint(x, pltpu.HBM) for x in (basis_in, basis_out)])


def rotate_kernel(count, *refs):
    firsts, seconds = refs[:count], refs[count : 2 * count]
    basis_in, basis_out, keep, send, rows = refs[2 * count :]
    own = core_id() == 0
    half = keep.shape[0]
    lo = 0
    for first, second in zip(firsts, seconds):
        a, b = first[...], second[...]
        hi = lo + a.shape[0]
        rows[lo:hi] = jnp.where(own, a, b)
        rows[half + lo : half + hi] = jnp.where(own, b, a)
        lo = hi
    width = basis_in.shape[1]
    tile = 256
    for basis, base in ((basis_in, 0), (basis_out, width)):
        columns = slice(base, base + basis.shape[1])
        for lo in range(0, basis.shape[0], tile):
            got = lax.dot_general(
                rows[:, columns],
                basis[lo : lo + tile],
                (((1,), (1,)), ((), ())),
                preferred_element_type=jnp.float32,
            )
            keep[:, base + lo : base + lo + tile] = got[:half]
            send[:, base + lo : base + lo + tile] = got[half:]


def rotate(firsts, seconds, basis_in, basis_out):
    count = len(firsts)
    half, width = sum(x.shape[0] for x in firsts), firsts[0].shape[1]
    shape = jax.ShapeDtypeStruct((half, width), jnp.float32)
    return pl.pallas_call(
        functools.partial(rotate_kernel, count),
        in_specs=[VMEM] * (2 * count + 2),
        out_specs=[VMEM] * 2,
        out_shape=[shape, shape],
        scratch_shapes=[pltpu.VMEM((2 * half, width), jnp.bfloat16)],
        compiler_params=params(16),
        cost_estimate=pl.CostEstimate(
            flops=4 * half * (basis_in.size + basis_out.size),
            bytes_accessed=100_000,
            transcendentals=0,
        ),
    )(*firsts, *seconds, basis_in, basis_out)


def store_codes(total, in_width, store):
    side_in, side_out = total[:, :in_width], total[:, in_width:]
    level_in, level_out = level_of(side_in), level_of(side_out)
    store(0, in_width, encode(side_in, level_in))
    store(in_width, total.shape[1], encode(side_out, level_out))
    store(total.shape[1], total.shape[1] + PAD, pack_levels(level_in, level_out))


def code_kernel(in_width, keep, got, *refs):
    done, out = refs[:-1], refs[-1]
    slot = 0
    for codes in done:
        out[slot : slot + codes.shape[0]] = codes[...]
        slot += codes.shape[0]
    for part in range(keep.shape[0] // RANK):
        rows = slice(part * RANK, (part + 1) * RANK)

        def store(lo, hi, value, slot=slot + part):
            out[slot, :, lo:hi] = value

        store_codes(keep[rows] + got[rows], in_width, store)


def code(keep, got, in_width, *done):
    slots = keep.shape[0] // RANK + sum(codes.shape[0] for codes in done)
    return pl.pallas_call(
        functools.partial(code_kernel, in_width),
        in_specs=[VMEM] * (2 + len(done)),
        out_specs=VMEM,
        out_shape=jax.ShapeDtypeStruct((slots, RANK, keep.shape[1] + PAD), jnp.int16),
        compiler_params=params(16),
        cost_estimate=BRIEF,
    )(keep, got, *done)


def resum_kernel(in_width, codes, out):
    width = codes.shape[2] - PAD
    total_in = total_out = 0.0
    for source in range(codes.shape[0]):
        unit_in, unit_out = units(codes[source, :, width:])
        total_in += as_float(codes[source, :, :in_width]) * unit_in
        total_out += as_float(codes[source, :, in_width:width]) * unit_out

    def store(lo, hi, value):
        for target in range(out.shape[0]):
            out[target, :, lo:hi] = value

    store_codes(jnp.concatenate([total_in, total_out], axis=1), in_width, store)


def resum(codes, in_width):
    return pl.pallas_call(
        functools.partial(resum_kernel, in_width),
        in_specs=[VMEM],
        out_specs=VMEM,
        out_shape=jax.ShapeDtypeStruct(codes.shape, jnp.int16),
        compiler_params=params(24),
    )(codes)


def project_kernel(is_own, *refs):
    codes, acts, grads, out = refs[0], refs[1], refs[2], refs[-1]
    half = core_id() if is_own else 1 - core_id()
    place = lax.axis_index("inp")
    x_lo, z = place // 8, lax.rem(place, 8)
    in_width, tokens = acts.shape[1], acts.shape[0]
    width = codes.shape[2] - PAD
    contract = (((1,), (1,)), ((), ()))

    def side(codes, unit, data):
        value = as_float(codes)
        high = value.astype(jnp.bfloat16)
        low = (value - high.astype(jnp.float32)).astype(jnp.bfloat16)
        data = data[...]
        got = lax.dot_general(high, data, contract, preferred_element_type=jnp.float32)
        got += lax.dot_general(low, data, contract, preferred_element_type=jnp.float32)
        return got * unit

    rows = codes.shape[0] * RANK
    unit_in, unit_out = units(codes[:, :, width:].reshape(rows, PAD))
    side_in = side(codes[:, :, :in_width].reshape(rows, in_width), unit_in, acts)
    side_out = side(codes[:, :, in_width:width].reshape(rows, width - in_width), unit_out, grads)
    level_in, level_out = level_of(side_in), level_of(side_out)
    code_in, code_out = encode(side_in, level_in), encode(side_out, level_out)
    tail = pack_levels(level_in, level_out)
    sign = 2 * half - 1
    for slot in range(8):
        away = (slot + 1) // 2
        cross = (slot + 1) % 2 if 0 < slot < 7 else half
        target = lax.rem(x_lo + cross, 2) * 8 + lax.rem(z + sign * away + 8, 8)
        span = slice(slot * RANK, (slot + 1) * RANK)
        out[target, :, 0:tokens] = code_in[span]
        out[target, :, tokens : 2 * tokens] = code_out[span]
        out[target, :, 2 * tokens :] = tail[span]


def project(codes, acts, grads, *filled):
    tokens = acts.shape[0]
    return pl.pallas_call(
        functools.partial(project_kernel, not filled),
        in_specs=[VMEM] * (3 + len(filled)),
        out_specs=VMEM,
        out_shape=jax.ShapeDtypeStruct((16, RANK, 2 * tokens + PAD), jnp.int16),
        input_output_aliases={3: 0} if filled else {},
        compiler_params=params(40),
        cost_estimate=BRIEF,
    )(codes, acts, grads, *filled)


def score_kernel(lengths, codes, out):
    tokens = (codes.shape[2] - PAD) // 2
    side_in = side_out = 0.0
    for source in range(codes.shape[0]):
        unit_in, unit_out = units(codes[source, :, 2 * tokens :])
        side_in += as_float(codes[source, :, :tokens]) * unit_in
        side_out += as_float(codes[source, :, tokens : 2 * tokens]) * unit_out
    per_token = jnp.sum(side_in * side_out, axis=0, keepdims=True)
    position = lax.axis_index("out") * tokens + lax.broadcasted_iota(jnp.int32, (1, tokens), 1)
    lane = lax.broadcasted_iota(jnp.int32, (1, 128), 1)
    sums = jnp.zeros((1, 128), jnp.float32)
    start = jnp.int32(0)
    for example in range(lengths.shape[0]):
        finish = start + lengths[example]
        inside = (position >= start) & (position < finish)
        total = jnp.sum(jnp.where(inside, per_token, 0.0), axis=1, keepdims=True)
        sums = jnp.where(lane == example, total, sums)
        start = finish
    for target in range(out.shape[0]):
        out[target] = jnp.broadcast_to(sums, out.shape[1:])


def score(lengths, codes):
    return pl.pallas_call(
        score_kernel,
        in_specs=[SMEM, VMEM],
        out_specs=VMEM,
        out_shape=jax.ShapeDtypeStruct((16, 8, 128), jnp.float32),
        compiler_params=params(16),
    )(lengths, codes)


UP = [(x * 8 + z, x * 8 + (z + 1) % 8) for x in range(2) for z in range(8)]
DOWN = [(b, a) for a, b in UP]
ACROSS = [(i, (i + 8) % 16) for i in range(16)]
CORES = [(i, i ^ 1) for i in range(16)]
CHIPS = [[2 * chip + core for chip in range(8)] for core in range(2)]


def per_device(acts, grads, basis_in, basis_out, query_in, query_out, lengths):
    in_width = basis_in.shape[0]
    mine = jnp.concatenate([query_in.T, query_out.T], axis=1)
    other = lax.ppermute(mine, "inp", ACROSS)


    def hop(ends):
        up, down = ends
        return lax.ppermute(up, "inp", UP), lax.ppermute(down, "inp", DOWN)

    def rotated(*ends):
        firsts, seconds = zip(*ends)
        return rotate(firsts, seconds, basis_in, basis_out)

    def finish(rotated, *done):
        keep, send = rotated
        return code(keep, lax.ppermute(send, "out", CORES), in_width, *done)

    a1 = hop((mine, mine))
    b1 = hop((other, other))
    a2 = hop(a1)
    b2 = hop(b1)
    b2, basis_in, basis_out = lax.optimization_barrier(
        (b2, *stage(basis_in, basis_out))
    )
    basis_in = pltpu.with_memory_space_constraint(basis_in, pltpu.VMEM)
    basis_out = pltpu.with_memory_space_constraint(basis_out, pltpu.VMEM)
    a3 = hop(a2)
    b3 = hop(b2)
    a4 = lax.ppermute(a3[0], "inp", UP)
    b4 = lax.ppermute(b3[1], "inp", DOWN)
    keep, send = rotated((mine, other), a1, b1, a2, b2, a3, b3)
    send, a4, b4 = lax.optimization_barrier((send, a4, b4))
    end = rotated((a4, b4))
    codes = finish(end, finish((keep, send)))
    codes = lax.all_to_all(codes, "out", 0, 0, tiled=True, axis_index_groups=CHIPS)
    codes = resum(codes, in_width)
    own = lax.all_to_all(codes, "out", 0, 0, tiled=True, axis_index_groups=CHIPS)
    sibling = lax.ppermute(own, "out", CORES)
    sides = project(sibling, acts, grads, project(own, acts, grads))
    sides = lax.all_to_all(sides, "inp", 0, 0, tiled=True)
    sums = score(lengths, sides)
    sums = lax.all_to_all(sums, "out", 0, 0, tiled=True)
    total = jnp.sum(sums[:, 0, : lengths.shape[0]], axis=0)
    return (total / lengths.astype(jnp.float32))[:, None]


def solution(mesh):
    placed = (
        P("out", "inp"),
        P("out", "inp"),
        P("inp", "out"),
        P("inp", "out"),
        P("out", "inp"),
        P("out", "inp"),
        P(),
    )
    return jax.shard_map(
        per_device, mesh=mesh, in_specs=placed, out_specs=P(None, "inp"), check_vma=False
    )
```
